32 devices in a mesh: replica: 2 (over x), pool: 16 (over z, y, core).
Axes of the slice: x: 2, y: 2, z: 4, core: 2. Of those that a mesh axis runs over, the one named last changes fastest.
Arguments:
- stretch_queries: bfloat16 [4096, 8192], P(('replica', 'pool')), parts along dimension 0, may hold values from -7 to 7
- decode_queries: bfloat16 [128, 8192], P(('replica', 'pool')), parts along dimension 0, may hold values from -7 to 7
- stretch_entries: bfloat16 [2, 4096, 1024], P(None, ('replica', 'pool')), parts along dimension 1, may hold values from -7 to 7
- decode_entries: bfloat16 [2, 128, 1024], P(None, ('replica', 'pool')), parts along dimension 1, may hold values from -7 to 7
- pool_pages: bfloat16 [2048, 2, 16, 1024], P(('replica', 'pool')), parts along dimension 0, may hold values from -7 to 7
- page_owner: int32 [3072, 1], P(('replica', 'pool')), parts along dimension 0, may hold values from 0 to 15; in each aligned block of 96 rows (0 to 95, 96 to 191, ...) at most 8 rows name the same one
- page_slot: int32 [3072], P(('replica', 'pool')), parts along dimension 0, may hold values from 0 to 63
- prefix_length: int32 [32], P(('replica', 'pool')), parts along dimension 0, may hold values from 0 to 768, as said below
- context_length: int32 [128], P(('replica', 'pool')), parts along dimension 0, may hold values from 1 to 192, as said below
Outputs:
- stretch_output: bfloat16 [4096, 8192], P(('replica', 'pool')), parts along dimension 0
- decode_output: bfloat16 [128, 8192], P(('replica', 'pool')), parts along dimension 0
The draws below stay inside these ranges and needn't reach their ends.
There are 2 independent parts, one for each index of `replica`. The reference program is written for one: setup_inputs(seed, part) draws one part's arguments, and reference() takes and returns one part's arrays. A program takes and returns all parts, laid end to end along the dimension named above; each array names one. Nothing has to cross between parts.
Inputs may be any that keep to these rules, and one draw needn't show every extreme that they name: `page_owner`: in the 96 rows of one device no owner appears more than 8 times; in some devices' rows one owner appears exactly 8 times. `prefix_length`: some batch shard has the full 48 * 16 prefix positions. `context_length`: some decode row has the full 12 * 16 positions.
All inputs are finite; a program needn't handle non-finite values.
Results may differ from the reference program's by a relative error of at most 0.0046.
Values may be sent and summed in bfloat16 or wider, within the bound.
A program may use at most 192 MiB of HBM per device.

```python
import math
import jax
import jax.numpy as jnp
import numpy as np
from jax import lax

HEADS = 64
KV_HEADS = 8
HEAD_DIM = 128
PAGE_TOKENS = 16
STRETCH = 128
DEC_ROWS = 4
PRE_PAGES = 48
DEC_PAGES = 12
SLOTS = 64
PAGES_DEV = 96
CAPACITY = 8
N_POOL = 16


def draw_stretch_queries(key, part):
    key = jax.random.fold_in(key, 101)
    row_count = N_POOL * STRETCH
    base = jnp.clip(jax.random.normal(key, (row_count, HEADS * HEAD_DIM)), -4.0, 4.0)
    return base.astype(jnp.bfloat16)


def draw_decode_queries(key, part):
    key = jax.random.fold_in(key, 102)
    row_count = N_POOL * DEC_ROWS
    base = jnp.clip(jax.random.normal(key, (row_count, HEADS * HEAD_DIM)), -4.0, 4.0)
    return base.astype(jnp.bfloat16)


def draw_stretch_entries(key, part):
    key = jax.random.fold_in(key, 103)
    row_count = N_POOL * STRETCH
    key_width = KV_HEADS * HEAD_DIM
    base = jnp.clip(jax.random.normal(key, (2, row_count, key_width)), -4.0, 4.0)
    return base.astype(jnp.bfloat16)


def draw_decode_entries(key, part):
    key = jax.random.fold_in(key, 104)
    row_count = N_POOL * DEC_ROWS
    key_width = KV_HEADS * HEAD_DIM
    base = jnp.clip(jax.random.normal(key, (2, row_count, key_width)), -4.0, 4.0)
    return base.astype(jnp.bfloat16)


def draw_pool_pages(key, part):
    key = jax.random.fold_in(key, 105)
    key_width = KV_HEADS * HEAD_DIM
    shape = (N_POOL * SLOTS, 2, PAGE_TOKENS, key_width)
    base = jnp.clip(jax.random.normal(key, shape), -4.0, 4.0)
    return base.astype(jnp.bfloat16)


def draw_prefix_length(key, part):
    key = jax.random.fold_in(key, 106)
    first, second = jax.random.split(key)
    longest = PRE_PAGES * PAGE_TOKENS
    lengths = jax.random.randint(first, (N_POOL,), 0, longest + 1)
    which = jax.random.randint(second, (), 0, N_POOL)
    return lengths.at[which].set(longest).astype(jnp.int32)


def draw_context_length(key, part):
    key = jax.random.fold_in(key, 107)
    first, second = jax.random.split(key)
    longest = DEC_PAGES * PAGE_TOKENS
    lengths = jax.random.randint(first, (N_POOL * DEC_ROWS,), 1, longest + 1)
    which = jax.random.randint(second, (), 0, N_POOL * DEC_ROWS)
    return lengths.at[which].set(longest).astype(jnp.int32)


def with_ends(array, rng, least, top_value):
    index_at = [jax.random.randint(jax.random.fold_in(rng, axis), (), 0, length) for axis, length in enumerate(array.shape)]
    widest = array.shape.index(max(array.shape))
    neighbour = index_at[:widest] + [(index_at[widest] + 1) % array.shape[widest]] + index_at[widest + 1:]
    return array.at[tuple(index_at)].set(least).at[tuple(neighbour)].set(top_value)


def assign_block(rng, own, number, rows, amount, top, most, skew):
    order = jax.random.permutation(rng, amount)
    packed, common = load_shares(amount, rows * top, most, skew, True), load_shares(amount, rows * top, most, skew, False)
    places = jnp.arange(amount)

    def named(sizes, turn):
        used = int((sizes > 0).sum())
        fixed = max(1, used // 4)
        moved = fixed + (places - fixed + turn * (used - fixed)) % max(1, amount - fixed)
        return jnp.zeros((amount,), jnp.int32).at[order[jnp.where(places < fixed, places, moved)]].set(jnp.asarray(sizes, jnp.int32))

    sizes = jnp.where(number % 4 == 0, named(packed, number // 4), named(common, number - number // 4 - 1))
    mixed = jax.random.permutation(jax.random.fold_in(own, 3), amount)
    donor, sink = mixed[0:amount // 2 * 2:2], mixed[1:amount // 2 * 2:2]
    slack = jnp.minimum(sizes[donor] - 1, most - sizes[sink]) // 2
    slack = jnp.where((donor == order[0]) | (sink == order[0]) | (sizes[sink] == 0), 0, jnp.maximum(slack, 0))
    moved = jax.random.randint(jax.random.fold_in(own, 4), (amount // 2,), 0, 1 << 20) % (slack + 1)
    sizes = sizes.at[donor].add(-moved).at[sink].add(moved)
    items = jnp.searchsorted(jnp.cumsum(sizes), jnp.arange(rows * top), side="right").astype(jnp.int32)
    table = items.reshape(top, rows).T
    table = table[jax.random.permutation(jax.random.fold_in(own, 1), rows)]
    turn = jax.random.randint(jax.random.fold_in(own, 2), (rows, 1), 0, top)
    return jnp.take_along_axis(table, (jnp.arange(top)[None, :] + turn) % top, axis=1)


def load_shares(count, total, most, slope, full):
    loads = [(1 << 20) // math.isqrt(rank ** slope) + 1 for rank in range(1, count + 1)]
    largest = most if full else min(most, max(-(-total // count), total * loads[0] // sum(loads)))
    least = 1 if total - largest >= count - 1 else 0
    holding, surplus = [largest] + [least] * (count - 1), total - largest - least * (count - 1)
    while surplus > 0:
        movable = [i for i in range(1, count) if holding[i] < largest] or [i for i in range(1, count) if holding[i] < most]
        whole, left = sum([loads[i] for i in movable]), surplus
        for i in movable:
            addition = min(most - holding[i], max(1, left * loads[i] // whole), surplus)
            holding[i] = holding[i] + addition
            surplus = surplus - addition
    return np.array(holding)


def setup_inputs(seed: int = 0, part: int = 0) -> dict:
    splits = jax.random.split(jax.random.key(seed), 10)
    part_keys = jax.random.split(jax.random.fold_in(splits[9], part), 10)
    stretch_queries = draw_stretch_queries(jax.random.fold_in(jax.random.fold_in(splits[9], part), 71), part)
    decode_queries = draw_decode_queries(jax.random.fold_in(jax.random.fold_in(splits[9], part), 71), part)
    stretch_entries = draw_stretch_entries(jax.random.fold_in(jax.random.fold_in(splits[9], part), 71), part)
    decode_entries = draw_decode_entries(jax.random.fold_in(jax.random.fold_in(splits[9], part), 71), part)
    pool_pages = draw_pool_pages(jax.random.fold_in(jax.random.fold_in(splits[9], part), 71), part)
    page_owner_keys = jax.random.split(jax.random.fold_in(part_keys[5], 1), (N_POOL * PAGES_DEV) // PAGES_DEV)
    page_owner_turns = jax.random.permutation(jax.random.fold_in(part_keys[5], 3), (N_POOL * PAGES_DEV) // PAGES_DEV)
    page_owner = jax.vmap(lambda own, number: assign_block(jax.random.fold_in(part_keys[5], 2), own, number, PAGES_DEV, N_POOL, 1, CAPACITY, 2))(page_owner_keys, page_owner_turns).reshape((N_POOL * PAGES_DEV, 1))
    page_slot = with_ends(jax.random.randint(part_keys[6], (N_POOL * PAGES_DEV,), 0, SLOTS), jax.random.fold_in(part_keys[6], 1), 0, SLOTS - 1).astype(jnp.int32)
    prefix_length = draw_prefix_length(jax.random.fold_in(jax.random.fold_in(splits[9], part), 71), part)
    context_length = draw_context_length(jax.random.fold_in(jax.random.fold_in(splits[9], part), 71), part)
    return dict(stretch_queries=stretch_queries, decode_queries=decode_queries, stretch_entries=stretch_entries, decode_entries=decode_entries, pool_pages=pool_pages, page_owner=page_owner, page_slot=page_slot, prefix_length=prefix_length, context_length=context_length)


def attend(queries, parts):
    row_count = queries.shape[0]
    key_heads = parts[0][0].shape[-1] // HEAD_DIM
    group_size = HEADS // key_heads
    factor = 1.0 / (HEAD_DIM ** 0.5)
    results = []
    for head_index in range(key_heads):
        lower = head_index * group_size * HEAD_DIM
        upper = lower + group_size * HEAD_DIM
        head_queries = queries[:, lower:upper].reshape(row_count, group_size, HEAD_DIM).astype(jnp.float32)
        scores = []
        for keys, values, usable in parts:
            key_part = keys[..., head_index * HEAD_DIM:(head_index + 1) * HEAD_DIM].astype(jnp.float32)
            if key_part.ndim == 2:
                score = jnp.einsum("rgd,ld->grl", head_queries, key_part)
            else:
                score = jnp.einsum("rgd,rld->grl", head_queries, key_part)
            scores.append(jnp.where(usable[None], score * factor, -jnp.inf))
        joined = jnp.concatenate(scores, axis=2)
        highest = jnp.max(joined, axis=2, keepdims=True)
        terms = jnp.exp(joined - highest)
        totals = jnp.sum(terms, axis=2)
        rounded = lax.optimization_barrier(terms.astype(jnp.bfloat16)).astype(jnp.float32)
        summed = jnp.zeros((row_count, group_size, HEAD_DIM), jnp.float32)
        offset = 0
        for keys, values, usable in parts:
            length = keys.shape[-2]
            weight_part = rounded[:, :, offset:offset + length]
            value_part = values[..., head_index * HEAD_DIM:(head_index + 1) * HEAD_DIM].astype(jnp.float32)
            if value_part.ndim == 2:
                summed = summed + jnp.einsum("grl,ld->rgd", weight_part, value_part)
            else:
                summed = summed + jnp.einsum("grl,rld->rgd", weight_part, value_part)
            offset = offset + length
        results.append((summed / jnp.transpose(totals)[:, :, None]).reshape(row_count, group_size * HEAD_DIM))
    return jnp.concatenate(results, axis=1).astype(jnp.bfloat16)


def reference(stretch_queries, decode_queries, stretch_entries, decode_entries, pool_pages, page_owner, page_slot, prefix_length, context_length):
    key_width = KV_HEADS * HEAD_DIM
    pool_rows = (page_owner[:, 0] * SLOTS + page_slot).astype(jnp.int32)
    prefix_span = PRE_PAGES * PAGE_TOKENS
    context_span = DEC_PAGES * PAGE_TOKENS
    causal = jnp.arange(STRETCH)[:, None] >= jnp.arange(STRETCH)[None, :]

    def shard(items):
        stretch_part, decode_part, stretch_new, decode_new, table_rows, prefix_count, context_counts = items
        fetched_pages = jnp.take(pool_pages, table_rows, axis=0)
        prefix_keys = fetched_pages[:PRE_PAGES, 0].reshape(prefix_span, key_width)
        prefix_values = fetched_pages[:PRE_PAGES, 1].reshape(prefix_span, key_width)
        prefix_usable = (jnp.arange(prefix_span) < prefix_count)[None, :]
        stretch_out = attend(stretch_part, [(stretch_new[0], stretch_new[1], causal), (prefix_keys, prefix_values, prefix_usable)])
        decode_pages = fetched_pages[PRE_PAGES:].reshape(DEC_ROWS, DEC_PAGES, 2, PAGE_TOKENS, key_width)
        cache_keys = decode_pages[:, :, 0].reshape(DEC_ROWS, context_span, key_width)
        cache_values = decode_pages[:, :, 1].reshape(DEC_ROWS, context_span, key_width)
        cache_usable = jnp.arange(context_span)[None, :] < context_counts[:, None]
        own_usable = jnp.ones((DEC_ROWS, 1), dtype=jnp.bool_)
        decode_out = attend(decode_part, [(decode_new[0][:, None, :], decode_new[1][:, None, :], own_usable), (cache_keys, cache_values, cache_usable)])
        return stretch_out, decode_out

    inputs = (
        stretch_queries.reshape(N_POOL, STRETCH, HEADS * HEAD_DIM),
        decode_queries.reshape(N_POOL, DEC_ROWS, HEADS * HEAD_DIM),
        jnp.transpose(stretch_entries.reshape(2, N_POOL, STRETCH, key_width), (1, 0, 2, 3)),
        jnp.transpose(decode_entries.reshape(2, N_POOL, DEC_ROWS, key_width), (1, 0, 2, 3)),
        pool_rows.reshape(N_POOL, PAGES_DEV),
        prefix_length,
        context_length.reshape(N_POOL, DEC_ROWS),
    )
    stretch_out, decode_out = lax.map(shard, inputs)
    return stretch_out.reshape(N_POOL * STRETCH, HEADS * HEAD_DIM), decode_out.reshape(N_POOL * DEC_ROWS, HEADS * HEAD_DIM)
```

```python
import functools
import math

import jax
import jax.numpy as jnp
from jax import lax
from jax.experimental import pallas as pl
from jax.experimental.pallas import tpu as pltpu
from jax.sharding import PartitionSpec as P

HEADS = 64
HEAD_DIM = 128
PRE_PAGES = 48
DEC_PAGES = 12
LOG2_SCALE = math.log2(math.e) / math.sqrt(HEAD_DIM)
CONTRACT_LAST = (((1,), (1,)), ((), ()))


def scores_of(queries, keys):
    return lax.dot_general(queries, keys, CONTRACT_LAST, preferred_element_type=jnp.float32)


def weigh(score_parts, value_parts):
    highest = functools.reduce(
        jnp.maximum, [jnp.max(s, axis=1, keepdims=True) for s in score_parts]
    )
    total = 0.0
    summed = 0.0
    for scores, values in zip(score_parts, value_parts):
        terms = jnp.exp2((scores - highest) * LOG2_SCALE)
        total = total + jnp.sum(terms, axis=1, keepdims=True)
        summed = summed + jnp.dot(
            terms.astype(jnp.bfloat16), values, preferred_element_type=jnp.float32
        )
    return summed / total


def attention_kernel(
    places, prefix_length, context_length,
    queries, decode_queries, entries, decode_entries, pages,
    output, decode_output, cache, sem,
):
    page_count, _, page_tokens, _ = cache.shape
    head = pl.program_id(0)
    row_count = queries.shape[0]
    group = queries.shape[1] // HEAD_DIM

    @pl.when(head == 0)
    def _():
        def fetch(t, carry):
            pltpu.make_async_copy(pages.at[places[t]], cache.at[t], sem).start()
            return carry

        lax.fori_loop(0, page_count, fetch, 0)
        pltpu.make_async_copy(cache, cache, sem).wait()

    columns = pl.ds(pl.multiple_of(head * HEAD_DIM, HEAD_DIM), HEAD_DIM)
    span = PRE_PAGES * page_tokens
    prefix_keys = cache[:PRE_PAGES, 0, :, columns].reshape(span, HEAD_DIM)
    prefix_values = cache[:PRE_PAGES, 1, :, columns].reshape(span, HEAD_DIM)
    position = lax.broadcasted_iota(jnp.int32, (1, span), 1)
    prefix_bias = jnp.where(position < prefix_length[0], 0.0, -jnp.inf)
    causal_bias = jnp.where(
        lax.broadcasted_iota(jnp.int32, (row_count, row_count), 0)
        >= lax.broadcasted_iota(jnp.int32, (row_count, row_count), 1),
        0.0,
        -jnp.inf,
    )
    own_keys = entries[0]
    own_values = entries[1]
    step = 4
    for start in range(0, group, step):
        stacked = jnp.concatenate(
            [queries[:, g * HEAD_DIM : (g + 1) * HEAD_DIM] for g in range(start, start + step)],
            axis=0,
        )
        own_scores = scores_of(stacked, own_keys).reshape(step, row_count, row_count)
        own_scores = (own_scores + causal_bias[None]).reshape(step * row_count, row_count)
        prefix_scores = scores_of(stacked, prefix_keys) + prefix_bias
        result = weigh([own_scores, prefix_scores], [own_values, prefix_values])
        result = result.astype(jnp.bfloat16)
        for g in range(step):
            output[:, (start + g) * HEAD_DIM : (start + g + 1) * HEAD_DIM] = result[
                g * row_count : (g + 1) * row_count
            ]

    context_span = (page_count - PRE_PAGES) * page_tokens
    row_span = DEC_PAGES * page_tokens
    context_keys = cache[PRE_PAGES:, 0, :, columns].reshape(context_span, HEAD_DIM)
    context_values = cache[PRE_PAGES:, 1, :, columns].reshape(context_span, HEAD_DIM)
    row_queries = decode_queries[0]
    shape = (row_queries.shape[0], context_span)
    row = lax.broadcasted_iota(jnp.int32, shape, 0) // group
    place = lax.broadcasted_iota(jnp.int32, shape, 1)
    usable = jnp.zeros(shape, jnp.bool_)
    for r in range(context_span // row_span):
        usable = usable | (
            (row == r) & (place >= r * row_span) & (place < r * row_span + context_length[r])
        )
    context_scores = jnp.where(usable, scores_of(row_queries, context_keys), -jnp.inf)
    new_scores = scores_of(row_queries, decode_entries[0])
    own = lax.broadcasted_iota(jnp.int32, new_scores.shape, 0) // group
    own = own == lax.broadcasted_iota(jnp.int32, new_scores.shape, 1)
    new_scores = jnp.where(own, new_scores, -jnp.inf)
    decode_output[0] = weigh(
        [new_scores, context_scores], [decode_entries[1], context_values]
    ).astype(jnp.bfloat16)


def attention(places, prefix_length, context_length, queries, decode_queries, entries,
              decode_entries, pages):
    row_count = queries.shape[0]
    decode_count = decode_queries.shape[0]
    key_heads = pages.shape[-1] // HEAD_DIM
    group = HEADS // key_heads
    page_count = places.shape[0]
    arranged = decode_queries.reshape(decode_count, key_heads, group, HEAD_DIM)
    arranged = jnp.transpose(arranged, (1, 0, 2, 3)).reshape(key_heads, -1, HEAD_DIM)
    padded = jnp.pad(decode_entries, ((0, 0), (0, -decode_count % 16), (0, 0)))
    output, decoded = pl.pallas_call(
        attention_kernel,
        grid_spec=pltpu.PrefetchScalarGridSpec(
            num_scalar_prefetch=3,
            grid=(key_heads,),
            in_specs=[
                pl.BlockSpec((row_count, group * HEAD_DIM), lambda h, *_: (0, h)),
                pl.BlockSpec((1,) + arranged.shape[1:], lambda h, *_: (h, 0, 0)),
                pl.BlockSpec((2, row_count, HEAD_DIM), lambda h, *_: (0, 0, h)),
                pl.BlockSpec((2, padded.shape[1], HEAD_DIM), lambda h, *_: (0, 0, h)),
                pl.BlockSpec(memory_space=pl.ANY),
            ],
            out_specs=[
                pl.BlockSpec((row_count, group * HEAD_DIM), lambda h, *_: (0, h)),
                pl.BlockSpec((1,) + arranged.shape[1:], lambda h, *_: (h, 0, 0)),
            ],
            scratch_shapes=[
                pltpu.VMEM((page_count,) + pages.shape[1:], pages.dtype),
                pltpu.SemaphoreType.DMA,
            ],
        ),
        out_shape=[
            jax.ShapeDtypeStruct(queries.shape, jnp.bfloat16),
            jax.ShapeDtypeStruct(arranged.shape, jnp.bfloat16),
        ],
        compiler_params=pltpu.CompilerParams(
            dimension_semantics=("arbitrary",), vmem_limit_bytes=40 * 1024 * 1024
        ),
        name="paged_attention",
    )(places, prefix_length, context_length, queries, arranged, entries, padded, pages)
    decoded = decoded.reshape(key_heads, decode_count, group, HEAD_DIM)
    decoded = jnp.transpose(decoded, (1, 0, 2, 3)).reshape(decode_queries.shape)
    return output, decoded


def on_device(
    stretch_queries,
    decode_queries,
    stretch_entries,
    decode_entries,
    pool_pages,
    page_owner,
    page_slot,
    prefix_length,
    context_length,
):
    pool_size = lax.axis_size("pool")
    page_count = page_slot.shape[0]
    capacity = max(2, 4 * page_count // (3 * pool_size))
    slot_total = pool_size * capacity
    owners = page_owner[:, 0]
    member = (owners[:, None] == jnp.arange(pool_size, dtype=jnp.int32)[None, :]).astype(jnp.int32)
    ranks = jnp.sum(jnp.cumsum(member, axis=0) * member, axis=1) - 1
    target = owners * capacity + ranks
    placed = target[:, None] == jnp.arange(slot_total, dtype=jnp.int32)[None, :]
    requests = jnp.sum(jnp.where(placed, page_slot[:, None], 0), axis=0).reshape(
        pool_size, capacity
    )
    incoming = lax.all_to_all(requests, "pool", split_axis=0, concat_axis=0, tiled=True)
    served = jnp.take(pool_pages, incoming.reshape(-1), axis=0).reshape(
        (pool_size, capacity) + pool_pages.shape[1:]
    )
    received = lax.all_to_all(served, "pool", split_axis=0, concat_axis=0, tiled=True)
    received = received.reshape((slot_total,) + pool_pages.shape[1:])
    return attention(
        target, prefix_length, context_length, stretch_queries, decode_queries,
        stretch_entries, decode_entries, received,
    )


def solution(mesh):
    rows = P(("replica", "pool"), None)
    entries = P(None, ("replica", "pool"), None)
    vector = P(("replica", "pool"))
    pages = P(("replica", "pool"), None, None, None)
    return jax.shard_map(
        on_device,
        mesh=mesh,
        in_specs=(rows, rows, entries, entries, pages, rows, vector, vector, vector),
        out_specs=(rows, rows),
        check_vma=False,
    )
```

```python
import functools
import math

import jax
import jax.numpy as jnp
from jax import lax
from jax.experimental import pallas as pl
from jax.experimental.pallas import tpu as pltpu
from jax.sharding import PartitionSpec as P

HEADS = 64
HEAD_DIM = 128
PRE_PAGES = 48
DEC_PAGES = 12
LOG2_SCALE = math.log2(math.e) / math.sqrt(HEAD_DIM)
PLANE = 4
MESH = pl.DeviceIdType.MESH
CONTRACT_LAST = (((1,), (1,)), ((), ()))


def scores_of(queries, keys):
    return lax.dot_general(queries, keys, CONTRACT_LAST, preferred_element_type=jnp.float32)


def weigh(score_parts, value_parts):
    highest = functools.reduce(
        jnp.maximum, [jnp.max(s, axis=1, keepdims=True) for s in score_parts]
    )
    total = 0.0
    summed = 0.0
    for scores, values in zip(score_parts, value_parts):
        terms = jnp.exp2((scores - highest) * LOG2_SCALE)
        total = total + jnp.sum(terms, axis=1, keepdims=True)
        summed = summed + jnp.dot(
            terms.astype(jnp.bfloat16), values, preferred_element_type=jnp.float32
        )
    return summed / total


def attention_kernel(
    places, prefix_length, context_length,
    queries, decode_queries, entries, decode_entries, pages,
    output, decode_output, cache, sem,
):
    page_count, _, page_tokens, _ = cache.shape
    head = pl.program_id(0)
    row_count = queries.shape[0]
    group = queries.shape[1] // HEAD_DIM

    @pl.when(head == 0)
    def _():
        def fetch(t, carry):
            pltpu.make_async_copy(pages.at[places[t]], cache.at[t], sem).start()
            return carry

        lax.fori_loop(0, page_count, fetch, 0)
        pltpu.make_async_copy(cache, cache, sem).wait()

    columns = pl.ds(pl.multiple_of(head * HEAD_DIM, HEAD_DIM), HEAD_DIM)
    span = PRE_PAGES * page_tokens
    prefix_keys = cache[:PRE_PAGES, 0, :, columns].reshape(span, HEAD_DIM)
    prefix_values = cache[:PRE_PAGES, 1, :, columns].reshape(span, HEAD_DIM)
    position = lax.broadcasted_iota(jnp.int32, (1, span), 1)
    prefix_bias = jnp.where(position < prefix_length[0], 0.0, -jnp.inf)
    causal_bias = jnp.where(
        lax.broadcasted_iota(jnp.int32, (row_count, row_count), 0)
        >= lax.broadcasted_iota(jnp.int32, (row_count, row_count), 1),
        0.0,
        -jnp.inf,
    )
    own_keys = entries[0]
    own_values = entries[1]
    step = 4
    for start in range(0, group, step):
        stacked = jnp.concatenate(
            [queries[:, g * HEAD_DIM : (g + 1) * HEAD_DIM] for g in range(start, start + step)],
            axis=0,
        )
        own_scores = scores_of(stacked, own_keys).reshape(step, row_count, row_count)
        own_scores = (own_scores + causal_bias[None]).reshape(step * row_count, row_count)
        prefix_scores = scores_of(stacked, prefix_keys) + prefix_bias
        result = weigh([own_scores, prefix_scores], [own_values, prefix_values])
        result = result.astype(jnp.bfloat16)
        for g in range(step):
            output[:, (start + g) * HEAD_DIM : (start + g + 1) * HEAD_DIM] = result[
                g * row_count : (g + 1) * row_count
            ]

    context_span = (page_count - PRE_PAGES) * page_tokens
    row_span = DEC_PAGES * page_tokens
    context_keys = cache[PRE_PAGES:, 0, :, columns].reshape(context_span, HEAD_DIM)
    context_values = cache[PRE_PAGES:, 1, :, columns].reshape(context_span, HEAD_DIM)
    row_queries = decode_queries[0]
    shape = (row_queries.shape[0], context_span)
    row = lax.broadcasted_iota(jnp.int32, shape, 0) // group
    place = lax.broadcasted_iota(jnp.int32, shape, 1)
    usable = jnp.zeros(shape, jnp.bool_)
    for r in range(context_span // row_span):
        usable = usable | (
            (row == r) & (place >= r * row_span) & (place < r * row_span + context_length[r])
        )
    context_scores = jnp.where(usable, scores_of(row_queries, context_keys), -jnp.inf)
    new_scores = scores_of(row_queries, decode_entries[0])
    own = lax.broadcasted_iota(jnp.int32, new_scores.shape, 0) // group
    own = own == lax.broadcasted_iota(jnp.int32, new_scores.shape, 1)
    new_scores = jnp.where(own, new_scores, -jnp.inf)
    decode_output[0] = weigh(
        [new_scores, context_scores], [decode_entries[1], context_values]
    ).astype(jnp.bfloat16)


def attention(places, prefix_length, context_length, queries, decode_queries, entries,
              decode_entries, pages):
    row_count = queries.shape[0]
    decode_count = decode_queries.shape[0]
    key_heads = pages.shape[-1] // HEAD_DIM
    group = HEADS // key_heads
    page_count = places.shape[0]
    arranged = decode_queries.reshape(decode_count, key_heads, group, HEAD_DIM)
    arranged = jnp.transpose(arranged, (1, 0, 2, 3)).reshape(key_heads, -1, HEAD_DIM)
    padded = jnp.pad(decode_entries, ((0, 0), (0, -decode_count % 16), (0, 0)))
    output, decoded = pl.pallas_call(
        attention_kernel,
        grid_spec=pltpu.PrefetchScalarGridSpec(
            num_scalar_prefetch=3,
            grid=(key_heads,),
            in_specs=[
                pl.BlockSpec((row_count, group * HEAD_DIM), lambda h, *_: (0, h)),
                pl.BlockSpec((1,) + arranged.shape[1:], lambda h, *_: (h, 0, 0)),
                pl.BlockSpec((2, row_count, HEAD_DIM), lambda h, *_: (0, 0, h)),
                pl.BlockSpec((2, padded.shape[1], HEAD_DIM), lambda h, *_: (0, 0, h)),
                pl.BlockSpec(memory_space=pl.ANY),
            ],
            out_specs=[
                pl.BlockSpec((row_count, group * HEAD_DIM), lambda h, *_: (0, h)),
                pl.BlockSpec((1,) + arranged.shape[1:], lambda h, *_: (h, 0, 0)),
            ],
            scratch_shapes=[
                pltpu.VMEM((page_count,) + pages.shape[1:], pages.dtype),
                pltpu.SemaphoreType.DMA,
            ],
        ),
        out_shape=[
            jax.ShapeDtypeStruct(queries.shape, jnp.bfloat16),
            jax.ShapeDtypeStruct(arranged.shape, jnp.bfloat16),
        ],
        compiler_params=pltpu.CompilerParams(
            dimension_semantics=("arbitrary",), vmem_limit_bytes=40 * 1024 * 1024
        ),
        name="paged_attention",
    )(places, prefix_length, context_length, queries, arranged, entries, padded, pages)
    decoded = decoded.reshape(key_heads, decode_count, group, HEAD_DIM)
    decoded = jnp.transpose(decoded, (1, 0, 2, 3)).reshape(decode_queries.shape)
    return output, decoded


def exchange_kernel(chunks, served, held, local_sem, far_send, far_recv, side_send, side_recv,
                    core_send, core_recv):
    plane_count = served.shape[0]
    me = lax.axis_index("pool")
    plane = me // PLANE
    within = me % PLANE
    side = within // 2
    core = within % 2
    side_device = plane * PLANE + (1 - side) * 2 + core
    core_device = plane * PLANE + side * 2 + (1 - core)

    barrier = pltpu.get_barrier_semaphore()
    for offset in range(1, plane_count):
        pl.semaphore_signal(
            barrier, inc=1,
            device_id={"pool": lax.rem(plane + offset, plane_count) * PLANE + within},
            device_id_type=MESH,
        )
    for device in (side_device, core_device):
        pl.semaphore_signal(barrier, inc=1, device_id={"pool": device}, device_id_type=MESH)
    pl.semaphore_wait(barrier, plane_count + 1)

    def far(offset, k):
        target = lax.rem(plane + offset, plane_count)
        return pltpu.make_async_remote_copy(
            src_ref=served.at[target, pl.ds(*chunks[k])],
            dst_ref=held.at[me, pl.ds(*chunks[k])],
            send_sem=far_send.at[offset, k],
            recv_sem=far_recv.at[offset, k],
            device_id={"pool": target * PLANE + within},
            device_id_type=MESH,
        )

    def spread(offset, k, other_side, to_core):
        source_plane = lax.rem(plane + plane_count - offset, plane_count)
        row = (1 - side) if other_side else side
        source = source_plane * PLANE + row * 2 + core
        if offset == 0 and not other_side:
            block = served.at[plane, pl.ds(*chunks[k])]
        else:
            block = held.at[source, pl.ds(*chunks[k])]
        if to_core:
            send, recv = core_send.at[int(other_side), offset, k], core_recv.at[int(other_side), offset, k]
        else:
            send, recv = side_send.at[offset, k], side_recv.at[offset, k]
        return pltpu.make_async_remote_copy(
            src_ref=block,
            dst_ref=held.at[source, pl.ds(*chunks[k])],
            send_sem=send,
            recv_sem=recv,
            device_id={"pool": core_device if to_core else side_device},
            device_id_type=MESH,
        )

    count = len(chunks)
    for k in range(count):
        for offset in range(1, plane_count):
            far(offset, k).start()
    mine = pltpu.make_async_copy(served.at[plane], held.at[me], local_sem)
    mine.start()
    for k in range(count):
        spread(0, k, False, False).start()
        spread(0, k, False, True).start()

    def forward(k):
        for offset in range(plane_count):
            spread(offset, k, False, False).wait_recv()
            spread(offset, k, True, True).start()

    for k in range(count):
        for offset in range(1, plane_count):
            far(offset, k).wait_recv()
            spread(offset, k, False, False).start()
            spread(offset, k, False, True).start()
        if k:
            forward(k - 1)
    forward(count - 1)
    for k in range(count):
        for offset in range(plane_count):
            if offset:
                far(offset, k).wait_send()
            spread(offset, k, False, False).wait_send()
            spread(offset, k, False, True).wait()
            spread(offset, k, True, True).wait()
    mine.wait()


def exchange(served, pool_size, collective_id):
    plane_count, length = served.shape[:2]
    pieces = max(1, min(5, 20 // plane_count, length))
    edges = [length * k // pieces for k in range(pieces + 1)]
    chunks = [(low, high - low) for low, high in zip(edges, edges[1:])]
    one = pltpu.SemaphoreType.DMA((plane_count, pieces))
    two = pltpu.SemaphoreType.DMA((2, plane_count, pieces))
    return pl.pallas_call(
        functools.partial(exchange_kernel, chunks),
        out_shape=jax.ShapeDtypeStruct((pool_size,) + served.shape[1:], served.dtype),
        in_specs=[pl.BlockSpec(memory_space=pl.ANY)],
        out_specs=pl.BlockSpec(memory_space=pl.ANY),
        scratch_shapes=[pltpu.SemaphoreType.DMA, one, one, one, one, two, two],
        compiler_params=pltpu.CompilerParams(
            collective_id=collective_id, has_side_effects=True
        ),
        name="page_exchange",
    )(served)


def gather_kernel(slots, pages, served, sem):
    plane_count, length = served.shape[:2]

    def fetch(t, carry):
        for q in range(plane_count):
            pltpu.make_async_copy(pages.at[slots[q, t]], served.at[q, t], sem).start()
        return carry

    lax.fori_loop(0, length, fetch, 0)
    pltpu.make_async_copy(served, served, sem).wait()


def gather(slots, pages):
    return pl.pallas_call(
        gather_kernel,
        grid_spec=pltpu.PrefetchScalarGridSpec(
            num_scalar_prefetch=1,
            grid=(1,),
            in_specs=[pl.BlockSpec(memory_space=pl.ANY)],
            out_specs=pl.BlockSpec(memory_space=pl.ANY),
            scratch_shapes=[pltpu.SemaphoreType.DMA],
        ),
        out_shape=jax.ShapeDtypeStruct(slots.shape + pages.shape[1:], pages.dtype),
        name="gather_pages",
    )(slots, pages)


def on_device(
    stretch_queries,
    decode_queries,
    stretch_entries,
    decode_entries,
    pool_pages,
    page_owner,
    page_slot,
    prefix_length,
    context_length,
):
    pool_size = lax.axis_size("pool")
    parts = lax.axis_size("replica")
    part = lax.axis_index("replica")
    me = lax.axis_index("pool")
    plane_count = pool_size // PLANE
    page_count = page_slot.shape[0]
    slot_count, _, page_tokens, _ = pool_pages.shape
    capacity = max(2, 4 * page_count // (3 * pool_size))
    longest = min(slot_count, PLANE * capacity)

    first = jnp.concatenate(
        [jnp.arange(PRE_PAGES), jnp.tile(jnp.arange(DEC_PAGES), context_length.shape[0])]
    ).astype(jnp.int32) * page_tokens
    limit = jnp.concatenate(
        [
            jnp.broadcast_to(prefix_length, (PRE_PAGES,)),
            jnp.repeat(context_length, DEC_PAGES),
        ]
    )
    named = jnp.where(first < limit, page_owner[:, 0] * slot_count + page_slot, -1)
    everyone = lax.all_gather(named, ("replica", "pool"), tiled=True)
    everyone = everyone.reshape(parts * plane_count, PLANE * page_count, 1)
    every_page = jnp.arange(pool_size * slot_count, dtype=jnp.int32)
    needed = jnp.any(everyone == every_page, axis=1).astype(jnp.int32)
    needed = needed.reshape(parts, plane_count, pool_size, slot_count)
    most = jnp.max(jnp.sum(needed, axis=-1))
    needed = lax.dynamic_index_in_dim(needed, part, 0, keepdims=False)
    asked = lax.dynamic_index_in_dim(needed, me, 1, keepdims=False)
    asked_rank = jnp.where(asked == 1, jnp.cumsum(asked, axis=1) - 1, -1)
    coming = lax.dynamic_index_in_dim(needed, me // PLANE, 0, keepdims=False)
    coming_rank = (jnp.cumsum(coming, axis=1) - 1).reshape(-1)
    rank = jnp.sum(
        jnp.where(named[:, None] == every_page[None, :], coming_rank[None, :], 0), axis=1
    )
    slot_index = jnp.arange(slot_count, dtype=jnp.int32)
    slots = jnp.sum(
        jnp.where(
            asked_rank[:, None, :] == jnp.arange(longest, dtype=jnp.int32)[None, :, None],
            slot_index[None, None, :],
            0,
        ),
        axis=2,
    )
    lengths = sorted({-(-longest * share // 32) for share in (20, 21, 22, 24, 32)})

    def finish(length, collective_id):
        served = gather(slots[:, :length], pool_pages)
        held = exchange(served, pool_size, collective_id)
        held = held.reshape((pool_size * length,) + pool_pages.shape[1:])
        places = jnp.where(named >= 0, page_owner[:, 0] * length + rank, 0)
        return attention(
            places, prefix_length, context_length, stretch_queries, decode_queries,
            stretch_entries, decode_entries, held,
        )

    choice = sum((most > length).astype(jnp.int32) for length in lengths[:-1])
    return lax.switch(
        choice,
        [functools.partial(finish, length, index) for index, length in enumerate(lengths)],
    )


def solution(mesh):
    rows = P(("replica", "pool"), None)
    entries = P(None, ("replica", "pool"), None)
    vector = P(("replica", "pool"))
    pages = P(("replica", "pool"), None, None, None)
    return jax.shard_map(
        on_device,
        mesh=mesh,
        in_specs=(rows, rows, entries, entries, pages, rows, vector, vector, vector),
        out_specs=(rows, rows),
        check_vma=False,
    )
```

```python
import functools
import math

import jax
import jax.numpy as jnp
from jax import lax
from jax.experimental import pallas as pl
from jax.experimental.pallas import tpu as pltpu
from jax.sharding import PartitionSpec as P

HEADS = 64
HEAD_DIM = 128
PRE_PAGES = 48
DEC_PAGES = 12
LOG2_SCALE = math.log2(math.e) / math.sqrt(HEAD_DIM)
PLANE = 4
MESH = pl.DeviceIdType.MESH
CONTRACT_LAST = (((1,), (1,)), ((), ()))


def scores_of(queries, keys):
    return lax.dot_general(queries, keys, CONTRACT_LAST, preferred_element_type=jnp.float32)


def weigh(score_parts, value_parts):
    highest = functools.reduce(
        jnp.maximum, [jnp.max(s, axis=1, keepdims=True) for s in score_parts]
    )
    total = 0.0
    summed = 0.0
    for scores, values in zip(score_parts, value_parts):
        terms = jnp.exp2((scores - highest) * LOG2_SCALE)
        total = total + jnp.sum(terms, axis=1, keepdims=True)
        summed = summed + jnp.dot(
            terms.astype(jnp.bfloat16), values, preferred_element_type=jnp.float32
        )
    return summed / total


def attention_kernel(
    places, prefix_length, context_length,
    queries, decode_queries, entries, decode_entries, pages, own_pages,
    output, decode_output, cache, sem,
):
    page_count, _, page_tokens, _ = cache.shape
    head = pl.program_id(0)
    row_count = queries.shape[0]
    group = queries.shape[1] // HEAD_DIM

    @pl.when(head == 0)
    def _():
        def fetch(t, carry):
            place = places[t]

            @pl.when(place >= 0)
            def _():
                pltpu.make_async_copy(pages.at[place], cache.at[t], sem).start()

            @pl.when(place < 0)
            def _():
                pltpu.make_async_copy(own_pages.at[-1 - place], cache.at[t], sem).start()

            return carry

        lax.fori_loop(0, page_count, fetch, 0)
        pltpu.make_async_copy(cache, cache, sem).wait()

    columns = pl.ds(pl.multiple_of(head * HEAD_DIM, HEAD_DIM), HEAD_DIM)
    span = PRE_PAGES * page_tokens
    prefix_keys = cache[:PRE_PAGES, 0, :, columns].reshape(span, HEAD_DIM)
    prefix_values = cache[:PRE_PAGES, 1, :, columns].reshape(span, HEAD_DIM)
    position = lax.broadcasted_iota(jnp.int32, (1, span), 1)
    prefix_bias = jnp.where(position < prefix_length[0], 0.0, -jnp.inf)
    causal_bias = jnp.where(
        lax.broadcasted_iota(jnp.int32, (row_count, row_count), 0)
        >= lax.broadcasted_iota(jnp.int32, (row_count, row_count), 1),
        0.0,
        -jnp.inf,
    )
    own_keys = entries[0]
    own_values = entries[1]
    step = 4
    for start in range(0, group, step):
        stacked = jnp.concatenate(
            [queries[:, g * HEAD_DIM : (g + 1) * HEAD_DIM] for g in range(start, start + step)],
            axis=0,
        )
        own_scores = scores_of(stacked, own_keys).reshape(step, row_count, row_count)
        own_scores = (own_scores + causal_bias[None]).reshape(step * row_count, row_count)
        prefix_scores = scores_of(stacked, prefix_keys) + prefix_bias
        result = weigh([own_scores, prefix_scores], [own_values, prefix_values])
        result = result.astype(jnp.bfloat16)
        for g in range(step):
            output[:, (start + g) * HEAD_DIM : (start + g + 1) * HEAD_DIM] = result[
                g * row_count : (g + 1) * row_count
            ]

    context_span = (page_count - PRE_PAGES) * page_tokens
    row_span = DEC_PAGES * page_tokens
    context_keys = cache[PRE_PAGES:, 0, :, columns].reshape(context_span, HEAD_DIM)
    context_values = cache[PRE_PAGES:, 1, :, columns].reshape(context_span, HEAD_DIM)
    row_queries = decode_queries[0]
    shape = (row_queries.shape[0], context_span)
    row = lax.broadcasted_iota(jnp.int32, shape, 0) // group
    place = lax.broadcasted_iota(jnp.int32, shape, 1)
    usable = jnp.zeros(shape, jnp.bool_)
    for r in range(context_span // row_span):
        usable = usable | (
            (row == r) & (place >= r * row_span) & (place < r * row_span + context_length[r])
        )
    context_scores = jnp.where(usable, scores_of(row_queries, context_keys), -jnp.inf)
    new_scores = scores_of(row_queries, decode_entries[0])
    own = lax.broadcasted_iota(jnp.int32, new_scores.shape, 0) // group
    own = own == lax.broadcasted_iota(jnp.int32, new_scores.shape, 1)
    new_scores = jnp.where(own, new_scores, -jnp.inf)
    decode_output[0] = weigh(
        [new_scores, context_scores], [decode_entries[1], context_values]
    ).astype(jnp.bfloat16)


def attention(places, prefix_length, context_length, queries, decode_queries, entries,
              decode_entries, pages, own_pages):
    row_count = queries.shape[0]
    decode_count = decode_queries.shape[0]
    key_heads = pages.shape[-1] // HEAD_DIM
    group = HEADS // key_heads
    page_count = places.shape[0]
    arranged = decode_queries.reshape(decode_count, key_heads, group, HEAD_DIM)
    arranged = jnp.transpose(arranged, (1, 0, 2, 3)).reshape(key_heads, -1, HEAD_DIM)
    padded = jnp.pad(decode_entries, ((0, 0), (0, -decode_count % 16), (0, 0)))
    output, decoded = pl.pallas_call(
        attention_kernel,
        grid_spec=pltpu.PrefetchScalarGridSpec(
            num_scalar_prefetch=3,
            grid=(key_heads,),
            in_specs=[
                pl.BlockSpec((row_count, group * HEAD_DIM), lambda h, *_: (0, h)),
                pl.BlockSpec((1,) + arranged.shape[1:], lambda h, *_: (h, 0, 0)),
                pl.BlockSpec((2, row_count, HEAD_DIM), lambda h, *_: (0, 0, h)),
                pl.BlockSpec((2, padded.shape[1], HEAD_DIM), lambda h, *_: (0, 0, h)),
                pl.BlockSpec(memory_space=pl.ANY),
                pl.BlockSpec(memory_space=pl.ANY),
            ],
            out_specs=[
                pl.BlockSpec((row_count, group * HEAD_DIM), lambda h, *_: (0, h)),
                pl.BlockSpec((1,) + arranged.shape[1:], lambda h, *_: (h, 0, 0)),
            ],
            scratch_shapes=[
                pltpu.VMEM((page_count,) + pages.shape[1:], pages.dtype),
                pltpu.SemaphoreType.DMA,
            ],
        ),
        out_shape=[
            jax.ShapeDtypeStruct(queries.shape, jnp.bfloat16),
            jax.ShapeDtypeStruct(arranged.shape, jnp.bfloat16),
        ],
        compiler_params=pltpu.CompilerParams(
            dimension_semantics=("arbitrary",), vmem_limit_bytes=40 * 1024 * 1024
        ),
        name="paged_attention",
    )(places, prefix_length, context_length, queries, arranged, entries, padded, pages, own_pages)
    decoded = decoded.reshape(key_heads, decode_count, group, HEAD_DIM)
    decoded = jnp.transpose(decoded, (1, 0, 2, 3)).reshape(decode_queries.shape)
    return output, decoded


def exchange_kernel(chunks, served, held, far_send, far_recv, side_send, side_recv, core_send,
                    core_recv):
    plane_count = served.shape[0]
    me = lax.axis_index("pool")
    plane = me // PLANE
    within = me % PLANE
    side = within // 2
    core = within % 2
    side_device = plane * PLANE + (1 - side) * 2 + core
    core_device = plane * PLANE + side * 2 + (1 - core)

    barrier = pltpu.get_barrier_semaphore()
    for offset in range(1, plane_count):
        pl.semaphore_signal(
            barrier, inc=1,
            device_id={"pool": lax.rem(plane + offset, plane_count) * PLANE + within},
            device_id_type=MESH,
        )
    for device in (side_device, core_device):
        pl.semaphore_signal(barrier, inc=1, device_id={"pool": device}, device_id_type=MESH)
    pl.semaphore_wait(barrier, plane_count + 1)

    def far(offset, k):
        target = lax.rem(plane + offset, plane_count)
        return pltpu.make_async_remote_copy(
            src_ref=served.at[target, pl.ds(*chunks[k])],
            dst_ref=held.at[me, pl.ds(*chunks[k])],
            send_sem=far_send.at[offset, k],
            recv_sem=far_recv.at[offset, k],
            device_id={"pool": target * PLANE + within},
            device_id_type=MESH,
        )

    def spread(offset, k, other_side, to_core):
        source_plane = lax.rem(plane + plane_count - offset, plane_count)
        row = (1 - side) if other_side else side
        source = source_plane * PLANE + row * 2 + core
        if offset == 0 and not other_side:
            block = served.at[plane, pl.ds(*chunks[k])]
        else:
            block = held.at[source, pl.ds(*chunks[k])]
        if to_core:
            send, recv = core_send.at[int(other_side), offset, k], core_recv.at[int(other_side), offset, k]
        else:
            send, recv = side_send.at[offset, k], side_recv.at[offset, k]
        return pltpu.make_async_remote_copy(
            src_ref=block,
            dst_ref=held.at[source, pl.ds(*chunks[k])],
            send_sem=send,
            recv_sem=recv,
            device_id={"pool": core_device if to_core else side_device},
            device_id_type=MESH,
        )

    count = len(chunks)
    for k in range(count):
        for offset in range(1, plane_count):
            far(offset, k).start()
    for k in range(count):
        spread(0, k, False, False).start()
        spread(0, k, False, True).start()

    def forward(k):
        for offset in range(plane_count):
            spread(offset, k, False, False).wait_recv()
            spread(offset, k, True, True).start()

    for k in range(count):
        for offset in range(1, plane_count):
            far(offset, k).wait_recv()
            spread(offset, k, False, False).start()
            spread(offset, k, False, True).start()
        if k:
            forward(k - 1)
    forward(count - 1)
    for k in range(count):
        for offset in range(plane_count):
            if offset:
                far(offset, k).wait_send()
            spread(offset, k, False, False).wait_send()
            spread(offset, k, False, True).wait()
            spread(offset, k, True, True).wait()


def exchange(served, pool_size, collective_id):
    plane_count, length = served.shape[:2]
    pieces = max(1, min(5, 20 // plane_count, length))
    edges = [length * k // pieces for k in range(pieces + 1)]
    chunks = [(low, high - low) for low, high in zip(edges, edges[1:])]
    one = pltpu.SemaphoreType.DMA((plane_count, pieces))
    two = pltpu.SemaphoreType.DMA((2, plane_count, pieces))
    return pl.pallas_call(
        functools.partial(exchange_kernel, chunks),
        out_shape=jax.ShapeDtypeStruct((pool_size,) + served.shape[1:], served.dtype),
        in_specs=[pl.BlockSpec(memory_space=pl.ANY)],
        out_specs=pl.BlockSpec(memory_space=pl.ANY),
        scratch_shapes=[one, one, one, one, two, two],
        compiler_params=pltpu.CompilerParams(
            collective_id=collective_id, has_side_effects=True
        ),
        name="page_exchange",
    )(served)


def gather_kernel(slots, pages, served, sem):
    target = pl.program_id(0)

    def fetch(t, carry):
        pltpu.make_async_copy(pages.at[slots[target, t]], served.at[0, t], sem).start()
        return carry

    lax.fori_loop(0, served.shape[1], fetch, 0)
    pltpu.make_async_copy(served, served, sem).wait()


def gather(slots, pages):
    block = (1, slots.shape[1]) + pages.shape[1:]
    return pl.pallas_call(
        gather_kernel,
        grid_spec=pltpu.PrefetchScalarGridSpec(
            num_scalar_prefetch=1,
            grid=slots.shape[:1],
            in_specs=[pl.BlockSpec(memory_space=pl.ANY)],
            out_specs=pl.BlockSpec(block, lambda q, *_: (q, 0, 0, 0, 0)),
            scratch_shapes=[pltpu.SemaphoreType.DMA],
        ),
        out_shape=jax.ShapeDtypeStruct(slots.shape + pages.shape[1:], pages.dtype),
        compiler_params=pltpu.CompilerParams(
            dimension_semantics=("arbitrary",), vmem_limit_bytes=24 * 1024 * 1024
        ),
        name="gather_pages",
    )(slots, pages)


def tables_kernel(table, tables, local_sem, part_send, part_recv, far_send, far_recv, near_send,
                  near_recv):
    parts, plane_count = tables.shape[1:3]
    part = lax.axis_index("replica")
    me = lax.axis_index("pool")
    plane = me // PLANE
    within = me % PLANE

    def other_part(offset):
        return {"replica": lax.rem(part + offset, parts), "pool": me}

    def other_plane(offset):
        return {"pool": lax.rem(plane + offset, plane_count) * PLANE + within}

    def other_place(offset):
        return {"pool": plane * PLANE + lax.rem(within + offset, PLANE)}

    barrier = pltpu.get_barrier_semaphore()
    stages = [(other_part, parts), (other_plane, plane_count), (other_place, PLANE)]
    for device_of, size in stages:
        for offset in range(1, size):
            pl.semaphore_signal(
                barrier, inc=1, device_id=device_of(offset), device_id_type=MESH
            )
    pl.semaphore_wait(barrier, parts + plane_count + PLANE - 3)
    mine = pltpu.make_async_copy(table, tables.at[within, part, plane], local_sem)
    mine.start()
    mine.wait()
    blocks = [
        tables.at[within, part, plane],
        tables.at[within, pl.ds(0, parts), plane],
        tables.at[within],
    ]
    sems = [(part_send, part_recv), (far_send, far_recv), (near_send, near_recv)]
    for (device_of, size), block, (send, recv) in zip(stages, blocks, sems):
        copies = [
            pltpu.make_async_remote_copy(
                src_ref=block,
                dst_ref=block,
                send_sem=send.at[offset],
                recv_sem=recv.at[offset],
                device_id=device_of(offset),
                device_id_type=MESH,
            )
            for offset in range(1, size)
        ]
        for copy in copies:
            copy.start()
        for copy in copies:
            copy.wait()


def gather_tables(named, parts, plane_count, collective_id):
    width = -(-named.shape[0] // 128) * 128
    table = jnp.pad(named, (0, width - named.shape[0]), constant_values=-1)[None, :]
    sems = [pltpu.SemaphoreType.DMA]
    for size in (parts, plane_count, PLANE):
        sems += [pltpu.SemaphoreType.DMA((size,))] * 2
    return pl.pallas_call(
        tables_kernel,
        out_shape=jax.ShapeDtypeStruct((PLANE, parts, plane_count, 1, width), jnp.int32),
        in_specs=[pl.BlockSpec(memory_space=pltpu.VMEM)],
        out_specs=pl.BlockSpec(memory_space=pltpu.VMEM),
        scratch_shapes=sems,
        compiler_params=pltpu.CompilerParams(
            collective_id=collective_id, has_side_effects=True
        ),
        name="gather_tables",
    )(table)


def on_device(
    stretch_queries,
    decode_queries,
    stretch_entries,
    decode_entries,
    pool_pages,
    page_owner,
    page_slot,
    prefix_length,
    context_length,
):
    pool_size = lax.axis_size("pool")
    parts = lax.axis_size("replica")
    part = lax.axis_index("replica")
    me = lax.axis_index("pool")
    plane_count = pool_size // PLANE
    page_count = page_slot.shape[0]
    slot_count, _, page_tokens, _ = pool_pages.shape
    capacity = max(2, 4 * page_count // (3 * pool_size))
    longest = min(slot_count, PLANE * capacity)

    first = jnp.concatenate(
        [jnp.arange(PRE_PAGES), jnp.tile(jnp.arange(DEC_PAGES), context_length.shape[0])]
    ).astype(jnp.int32) * page_tokens
    limit = jnp.concatenate(
        [
            jnp.broadcast_to(prefix_length, (PRE_PAGES,)),
            jnp.repeat(context_length, DEC_PAGES),
        ]
    )
    named = jnp.where(first < limit, page_owner[:, 0] * slot_count + page_slot, -1)
    everyone = gather_tables(named, parts, plane_count, 0)
    everyone = jnp.transpose(everyone, (1, 2, 0, 3, 4))
    everyone = everyone.reshape(parts * plane_count, -1, 1)
    every_page = jnp.arange(pool_size * slot_count, dtype=jnp.int32)
    needed = jnp.any(everyone == every_page, axis=1).astype(jnp.int32)
    needed = needed.reshape(parts, plane_count, pool_size, slot_count)
    most = jnp.max(jnp.sum(needed, axis=-1))
    needed = lax.dynamic_index_in_dim(needed, part, 0, keepdims=False)
    asked = lax.dynamic_index_in_dim(needed, me, 1, keepdims=False)
    asked_rank = jnp.where(asked == 1, jnp.cumsum(asked, axis=1) - 1, -1)
    coming = lax.dynamic_index_in_dim(needed, me // PLANE, 0, keepdims=False)
    coming_rank = (jnp.cumsum(coming, axis=1) - 1).reshape(-1)
    rank = jnp.sum(
        jnp.where(named[:, None] == every_page[None, :], coming_rank[None, :], 0), axis=1
    )
    slot_index = jnp.arange(slot_count, dtype=jnp.int32)
    slots = jnp.sum(
        jnp.where(
            asked_rank[:, None, :] == jnp.arange(longest, dtype=jnp.int32)[None, :, None],
            slot_index[None, None, :],
            0,
        ),
        axis=2,
    )
    lengths = sorted({-(-longest * share // 32) for share in (20, 21, 22, 24, 32)})

    def finish(length, collective_id):
        served = gather(slots[:, :length], pool_pages)
        held = exchange(served, pool_size, collective_id)
        held = held.reshape((pool_size * length,) + pool_pages.shape[1:])
        owner = page_owner[:, 0]
        places = jnp.where(owner == me, -1 - page_slot, owner * length + rank)
        places = jnp.where(named >= 0, places, -1)
        return attention(
            places, prefix_length, context_length, stretch_queries, decode_queries,
            stretch_entries, decode_entries, held, pool_pages,
        )

    choice = sum((most > length).astype(jnp.int32) for length in lengths[:-1])
    return lax.switch(
        choice,
        [functools.partial(finish, length, index + 1) for index, length in enumerate(lengths)],
    )


def solution(mesh):
    rows = P(("replica", "pool"), None)
    entries = P(None, ("replica", "pool"), None)
    vector = P(("replica", "pool"))
    pages = P(("replica", "pool"), None, None, None)
    return jax.shard_map(
        on_device,
        mesh=mesh,
        in_specs=(rows, rows, entries, entries, pages, rows, vector, vector, vector),
        out_specs=(rows, rows),
        check_vma=False,
    )
```

```python
import functools
import math

import jax
import jax.numpy as jnp
from jax import lax
from jax.experimental import pallas as pl
from jax.experimental.pallas import tpu as pltpu
from jax.sharding import PartitionSpec as P

HEADS = 64
HEAD_DIM = 128
PRE_PAGES = 48
DEC_PAGES = 12
LOG2_SCALE = math.log2(math.e) / math.sqrt(HEAD_DIM)
PLANE = 4
MESH = pl.DeviceIdType.MESH
CONTRACT_LAST = (((1,), (1,)), ((), ()))


def scores_of(queries, keys):
    return lax.dot_general(queries, keys, CONTRACT_LAST, preferred_element_type=jnp.float32)


def weigh(score_parts, value_parts):
    highest = functools.reduce(
        jnp.maximum, [jnp.max(s, axis=1, keepdims=True) for s in score_parts]
    )
    total = 0.0
    summed = 0.0
    for scores, values in zip(score_parts, value_parts):
        terms = jnp.exp2((scores - highest) * LOG2_SCALE)
        total = total + jnp.sum(terms, axis=1, keepdims=True)
        summed = summed + jnp.dot(
            terms.astype(jnp.bfloat16), values, preferred_element_type=jnp.float32
        )
    return summed / total


def attention_kernel(
    places, prefix_length, context_length,
    queries, decode_queries, entries, decode_entries, pages, own_pages,
    output, decode_output, cache, sem,
):
    page_count, _, page_tokens, _ = cache.shape
    head = pl.program_id(0)
    row_count = queries.shape[0]
    group = queries.shape[1] // HEAD_DIM

    @pl.when(head == 0)
    def _():
        def fetch(t, carry):
            place = places[t]

            @pl.when(place >= 0)
            def _():
                pltpu.make_async_copy(pages.at[place], cache.at[t], sem).start()

            @pl.when(place < 0)
            def _():
                pltpu.make_async_copy(own_pages.at[-1 - place], cache.at[t], sem).start()

            return carry

        lax.fori_loop(0, page_count, fetch, 0)
        pltpu.make_async_copy(cache, cache, sem).wait()

    columns = pl.ds(pl.multiple_of(head * HEAD_DIM, HEAD_DIM), HEAD_DIM)
    span = PRE_PAGES * page_tokens
    prefix_keys = cache[:PRE_PAGES, 0, :, columns].reshape(span, HEAD_DIM)
    prefix_values = cache[:PRE_PAGES, 1, :, columns].reshape(span, HEAD_DIM)
    position = lax.broadcasted_iota(jnp.int32, (1, span), 1)
    prefix_bias = jnp.where(position < prefix_length[0], 0.0, -jnp.inf)
    causal_bias = jnp.where(
        lax.broadcasted_iota(jnp.int32, (row_count, row_count), 0)
        >= lax.broadcasted_iota(jnp.int32, (row_count, row_count), 1),
        0.0,
        -jnp.inf,
    )
    own_keys = entries[0]
    own_values = entries[1]
    step = 4
    for start in range(0, group, step):
        stacked = jnp.concatenate(
            [queries[:, g * HEAD_DIM : (g + 1) * HEAD_DIM] for g in range(start, start + step)],
            axis=0,
        )
        own_scores = scores_of(stacked, own_keys).reshape(step, row_count, row_count)
        own_scores = (own_scores + causal_bias[None]).reshape(step * row_count, row_count)
        prefix_scores = scores_of(stacked, prefix_keys) + prefix_bias
        result = weigh([own_scores, prefix_scores], [own_values, prefix_values])
        result = result.astype(jnp.bfloat16)
        for g in range(step):
            output[:, (start + g) * HEAD_DIM : (start + g + 1) * HEAD_DIM] = result[
                g * row_count : (g + 1) * row_count
            ]

    context_span = (page_count - PRE_PAGES) * page_tokens
    row_span = DEC_PAGES * page_tokens
    context_keys = cache[PRE_PAGES:, 0, :, columns].reshape(context_span, HEAD_DIM)
    context_values = cache[PRE_PAGES:, 1, :, columns].reshape(context_span, HEAD_DIM)
    row_queries = decode_queries[0]
    shape = (row_queries.shape[0], context_span)
    row = lax.broadcasted_iota(jnp.int32, shape, 0) // group
    place = lax.broadcasted_iota(jnp.int32, shape, 1)
    usable = jnp.zeros(shape, jnp.bool_)
    for r in range(context_span // row_span):
        usable = usable | (
            (row == r) & (place >= r * row_span) & (place < r * row_span + context_length[r])
        )
    context_scores = jnp.where(usable, scores_of(row_queries, context_keys), -jnp.inf)
    new_scores = scores_of(row_queries, decode_entries[0])
    own = lax.broadcasted_iota(jnp.int32, new_scores.shape, 0) // group
    own = own == lax.broadcasted_iota(jnp.int32, new_scores.shape, 1)
    new_scores = jnp.where(own, new_scores, -jnp.inf)
    decode_output[0] = weigh(
        [new_scores, context_scores], [decode_entries[1], context_values]
    ).astype(jnp.bfloat16)


def attention(places, prefix_length, context_length, queries, decode_queries, entries,
              decode_entries, pages, own_pages):
    row_count = queries.shape[0]
    decode_count = decode_queries.shape[0]
    key_heads = pages.shape[-1] // HEAD_DIM
    group = HEADS // key_heads
    page_count = places.shape[0]
    arranged = decode_queries.reshape(decode_count, key_heads, group, HEAD_DIM)
    arranged = jnp.transpose(arranged, (1, 0, 2, 3)).reshape(key_heads, -1, HEAD_DIM)
    padded = jnp.pad(decode_entries, ((0, 0), (0, -decode_count % 16), (0, 0)))
    output, decoded = pl.pallas_call(
        attention_kernel,
        grid_spec=pltpu.PrefetchScalarGridSpec(
            num_scalar_prefetch=3,
            grid=(key_heads,),
            in_specs=[
                pl.BlockSpec((row_count, group * HEAD_DIM), lambda h, *_: (0, h)),
                pl.BlockSpec((1,) + arranged.shape[1:], lambda h, *_: (h, 0, 0)),
                pl.BlockSpec((2, row_count, HEAD_DIM), lambda h, *_: (0, 0, h)),
                pl.BlockSpec((2, padded.shape[1], HEAD_DIM), lambda h, *_: (0, 0, h)),
                pl.BlockSpec(memory_space=pl.ANY),
                pl.BlockSpec(memory_space=pl.ANY),
            ],
            out_specs=[
                pl.BlockSpec((row_count, group * HEAD_DIM), lambda h, *_: (0, h)),
                pl.BlockSpec((1,) + arranged.shape[1:], lambda h, *_: (h, 0, 0)),
            ],
            scratch_shapes=[
                pltpu.VMEM((page_count,) + pages.shape[1:], pages.dtype),
                pltpu.SemaphoreType.DMA,
            ],
        ),
        out_shape=[
            jax.ShapeDtypeStruct(queries.shape, jnp.bfloat16),
            jax.ShapeDtypeStruct(arranged.shape, jnp.bfloat16),
        ],
        compiler_params=pltpu.CompilerParams(
            dimension_semantics=("arbitrary",), vmem_limit_bytes=40 * 1024 * 1024
        ),
        name="paged_attention",
    )(places, prefix_length, context_length, queries, arranged, entries, padded, pages, own_pages)
    decoded = decoded.reshape(key_heads, decode_count, group, HEAD_DIM)
    decoded = jnp.transpose(decoded, (1, 0, 2, 3)).reshape(decode_queries.shape)
    return output, decoded


def exchange_kernel(chunks, shared, served, held, far_send, far_recv, side_send, side_recv, core_send,
                    core_recv):
    plane_count = served.shape[0]
    me = lax.axis_index("pool")
    plane = me // PLANE
    within = me % PLANE
    side = within // 2
    core = within % 2
    side_device = plane * PLANE + (1 - side) * 2 + core
    core_device = plane * PLANE + side * 2 + (1 - core)

    barrier = pltpu.get_barrier_semaphore()
    for offset in range(1, plane_count):
        pl.semaphore_signal(
            barrier, inc=1,
            device_id={"pool": lax.rem(plane + offset, plane_count) * PLANE + within},
            device_id_type=MESH,
        )
    for device in (side_device, core_device):
        pl.semaphore_signal(barrier, inc=1, device_id={"pool": device}, device_id_type=MESH)
    pl.semaphore_wait(barrier, plane_count + 1)

    def far(offset, k):
        target = lax.rem(plane + offset, plane_count)
        return pltpu.make_async_remote_copy(
            src_ref=served.at[target, pl.ds(*chunks[k])],
            dst_ref=held.at[me, pl.ds(*chunks[k])],
            send_sem=far_send.at[offset, k],
            recv_sem=far_recv.at[offset, k],
            device_id={"pool": target * PLANE + within},
            device_id_type=MESH,
        )

    def spread(offset, k, other_side, to_core):
        source_plane = lax.rem(plane + plane_count - offset, plane_count)
        row = (1 - side) if other_side else side
        source = source_plane * PLANE + row * 2 + core
        if offset == 0 and not other_side:
            block = served.at[plane, pl.ds(*chunks[k])]
        else:
            block = held.at[source, pl.ds(*chunks[k])]
        if to_core:
            send, recv = core_send.at[int(other_side), offset, k], core_recv.at[int(other_side), offset, k]
        else:
            send, recv = side_send.at[offset, k], side_recv.at[offset, k]
        return pltpu.make_async_remote_copy(
            src_ref=block,
            dst_ref=held.at[source, pl.ds(*chunks[k])],
            send_sem=send,
            recv_sem=recv,
            device_id={"pool": core_device if to_core else side_device},
            device_id_type=MESH,
        )

    count = len(chunks)
    for k in range(count):
        for offset in range(1, plane_count):
            far(offset, k).start()
    for k in range(count):
        if k < shared:
            spread(0, k, False, False).start()
        spread(0, k, False, True).start()

    def forward(k):
        for offset in range(plane_count):
            spread(offset, k, False, False).wait_recv()
            spread(offset, k, True, True).start()

    for k in range(count):
        for offset in range(1, plane_count):
            far(offset, k).wait_recv()
            if k < shared:
                spread(offset, k, False, False).start()
            spread(offset, k, False, True).start()
        if 0 < k <= shared:
            forward(k - 1)
    if shared == count:
        forward(count - 1)
    for k in range(count):
        for offset in range(plane_count):
            if offset:
                far(offset, k).wait_send()
            spread(offset, k, False, True).wait()
            if k < shared:
                spread(offset, k, False, False).wait_send()
                spread(offset, k, True, True).wait()


def exchange(served, shared_length, pool_size, collective_id):
    plane_count, length = served.shape[:2]
    shared_length = min(shared_length, length)
    shared = max(1, min(5, 20 // plane_count, shared_length))
    edges = [shared_length * k // shared for k in range(shared + 1)]
    if length > shared_length:
        middle = (length + shared_length) // 2
        edges += [middle, length] if middle > shared_length else [length]
    chunks = [(low, high - low) for low, high in zip(edges, edges[1:])]
    pieces = len(chunks)
    one = pltpu.SemaphoreType.DMA((plane_count, pieces))
    two = pltpu.SemaphoreType.DMA((2, plane_count, pieces))
    return pl.pallas_call(
        functools.partial(exchange_kernel, chunks, shared),
        out_shape=jax.ShapeDtypeStruct((pool_size,) + served.shape[1:], served.dtype),
        in_specs=[pl.BlockSpec(memory_space=pl.ANY)],
        out_specs=pl.BlockSpec(memory_space=pl.ANY),
        scratch_shapes=[one, one, one, one, two, two],
        compiler_params=pltpu.CompilerParams(
            collective_id=collective_id, has_side_effects=True
        ),
        name="page_exchange",
    )(served)


def gather_kernel(slots, pages, served, sem):
    target = pl.program_id(0)

    def fetch(t, carry):
        pltpu.make_async_copy(pages.at[slots[target, t]], served.at[0, t], sem).start()
        return carry

    lax.fori_loop(0, served.shape[1], fetch, 0)
    pltpu.make_async_copy(served, served, sem).wait()


def gather(slots, pages):
    block = (1, slots.shape[1]) + pages.shape[1:]
    return pl.pallas_call(
        gather_kernel,
        grid_spec=pltpu.PrefetchScalarGridSpec(
            num_scalar_prefetch=1,
            grid=slots.shape[:1],
            in_specs=[pl.BlockSpec(memory_space=pl.ANY)],
            out_specs=pl.BlockSpec(block, lambda q, *_: (q, 0, 0, 0, 0)),
            scratch_shapes=[pltpu.SemaphoreType.DMA],
        ),
        out_shape=jax.ShapeDtypeStruct(slots.shape + pages.shape[1:], pages.dtype),
        compiler_params=pltpu.CompilerParams(
            dimension_semantics=("arbitrary",), vmem_limit_bytes=24 * 1024 * 1024
        ),
        name="gather_pages",
    )(slots, pages)


def tables_kernel(table, tables, local_sem, part_send, part_recv, far_send, far_recv, near_send,
                  near_recv):
    parts, plane_count = tables.shape[1:3]
    part = lax.axis_index("replica")
    me = lax.axis_index("pool")
    plane = me // PLANE
    within = me % PLANE

    def other_part(offset):
        return {"replica": lax.rem(part + offset, parts), "pool": me}

    def other_plane(offset):
        return {"pool": lax.rem(plane + offset, plane_count) * PLANE + within}

    def other_place(offset):
        return {"pool": plane * PLANE + lax.rem(within + offset, PLANE)}

    barrier = pltpu.get_barrier_semaphore()
    stages = [(other_part, parts), (other_plane, plane_count), (other_place, PLANE)]
    for device_of, size in stages:
        for offset in range(1, size):
            pl.semaphore_signal(
                barrier, inc=1, device_id=device_of(offset), device_id_type=MESH
            )
    pl.semaphore_wait(barrier, parts + plane_count + PLANE - 3)
    mine = pltpu.make_async_copy(table, tables.at[within, part, plane], local_sem)
    mine.start()
    mine.wait()
    blocks = [
        tables.at[within, part, plane],
        tables.at[within, pl.ds(0, parts), plane],
        tables.at[within],
    ]
    sems = [(part_send, part_recv), (far_send, far_recv), (near_send, near_recv)]
    for (device_of, size), block, (send, recv) in zip(stages, blocks, sems):
        copies = [
            pltpu.make_async_remote_copy(
                src_ref=block,
                dst_ref=block,
                send_sem=send.at[offset],
                recv_sem=recv.at[offset],
                device_id=device_of(offset),
                device_id_type=MESH,
            )
            for offset in range(1, size)
        ]
        for copy in copies:
            copy.start()
        for copy in copies:
            copy.wait()


def gather_tables(named, parts, plane_count, collective_id):
    width = -(-named.shape[0] // 128) * 128
    table = jnp.pad(named, (0, width - named.shape[0]), constant_values=-1)[None, :]
    sems = [pltpu.SemaphoreType.DMA]
    for size in (parts, plane_count, PLANE):
        sems += [pltpu.SemaphoreType.DMA((size,))] * 2
    return pl.pallas_call(
        tables_kernel,
        out_shape=jax.ShapeDtypeStruct((PLANE, parts, plane_count, 1, width), jnp.int32),
        in_specs=[pl.BlockSpec(memory_space=pltpu.VMEM)],
        out_specs=pl.BlockSpec(memory_space=pltpu.VMEM),
        scratch_shapes=sems,
        compiler_params=pltpu.CompilerParams(
            collective_id=collective_id, has_side_effects=True
        ),
        name="gather_tables",
    )(table)


def on_device(
    stretch_queries,
    decode_queries,
    stretch_entries,
    decode_entries,
    pool_pages,
    page_owner,
    page_slot,
    prefix_length,
    context_length,
):
    pool_size = lax.axis_size("pool")
    parts = lax.axis_size("replica")
    part = lax.axis_index("replica")
    me = lax.axis_index("pool")
    plane_count = pool_size // PLANE
    page_count = page_slot.shape[0]
    slot_count, _, page_tokens, _ = pool_pages.shape
    capacity = max(2, 4 * page_count // (3 * pool_size))
    longest = min(slot_count, PLANE * capacity)

    first = jnp.concatenate(
        [jnp.arange(PRE_PAGES), jnp.tile(jnp.arange(DEC_PAGES), context_length.shape[0])]
    ).astype(jnp.int32) * page_tokens
    limit = jnp.concatenate(
        [
            jnp.broadcast_to(prefix_length, (PRE_PAGES,)),
            jnp.repeat(context_length, DEC_PAGES),
        ]
    )
    named = jnp.where(first < limit, page_owner[:, 0] * slot_count + page_slot, -1)
    everyone = gather_tables(named, parts, plane_count, 0)
    everyone = jnp.transpose(everyone, (1, 2, 0, 3, 4))
    everyone = everyone.reshape(parts * plane_count * 2, -1, 1)
    every_page = jnp.arange(pool_size * slot_count, dtype=jnp.int32)
    by_side = jnp.any(everyone == every_page, axis=1)
    by_side = by_side.reshape(parts, plane_count, 2, pool_size, slot_count)
    needed = (by_side[:, :, 0] | by_side[:, :, 1]).astype(jnp.int32)
    most = jnp.max(jnp.sum(needed, axis=-1))
    by_side = lax.dynamic_index_in_dim(by_side, part, 0, keepdims=False).astype(jnp.int32)
    source_side = (jnp.arange(pool_size)[:, None] // 2) % 2
    early = jnp.where(source_side == 0, by_side[:, 1], by_side[:, 0])
    late = jnp.maximum(by_side[:, 0], by_side[:, 1]) - early

    def ranked(early, late):
        early_rank = jnp.cumsum(early, axis=1) - 1
        late_rank = jnp.cumsum(late, axis=1) - 1 + jnp.sum(early, axis=1, keepdims=True)
        return jnp.where(early == 1, early_rank, jnp.where(late == 1, late_rank, -1))

    asked_rank = ranked(
        lax.dynamic_index_in_dim(early, me, 1, keepdims=False),
        lax.dynamic_index_in_dim(late, me, 1, keepdims=False),
    )
    plane = me // PLANE
    coming_rank = ranked(
        lax.dynamic_index_in_dim(early, plane, 0, keepdims=False),
        lax.dynamic_index_in_dim(late, plane, 0, keepdims=False),
    ).reshape(-1)
    rank = jnp.sum(
        jnp.where(named[:, None] == every_page[None, :], coming_rank[None, :], 0), axis=1
    )
    slot_index = jnp.arange(slot_count, dtype=jnp.int32)
    slots = jnp.sum(
        jnp.where(
            asked_rank[:, None, :] == jnp.arange(longest, dtype=jnp.int32)[None, :, None],
            slot_index[None, None, :],
            0,
        ),
        axis=2,
    )
    lengths = sorted({-(-longest * share // 32) for share in (20, 21, 22, 24, 32)})

    def finish(length, collective_id):
        served = gather(slots[:, :length], pool_pages)
        held = exchange(served, 2 * capacity, pool_size, collective_id)
        held = held.reshape((pool_size * length,) + pool_pages.shape[1:])
        owner = page_owner[:, 0]
        places = jnp.where(owner == me, -1 - page_slot, owner * length + rank)
        places = jnp.where(named >= 0, places, -1)
        return attention(
            places, prefix_length, context_length, stretch_queries, decode_queries,
            stretch_entries, decode_entries, held, pool_pages,
        )

    choice = sum((most > length).astype(jnp.int32) for length in lengths[:-1])
    return lax.switch(
        choice,
        [functools.partial(finish, length, index + 1) for index, length in enumerate(lengths)],
    )


def solution(mesh):
    rows = P(("replica", "pool"), None)
    entries = P(None, ("replica", "pool"), None)
    vector = P(("replica", "pool"))
    pages = P(("replica", "pool"), None, None, None)
    return jax.shard_map(
        on_device,
        mesh=mesh,
        in_specs=(rows, rows, entries, entries, pages, rows, vector, vector, vector),
        out_specs=(rows, rows),
        check_vma=False,
    )
```

```python
import functools
import math

import jax
import jax.numpy as jnp
from jax import lax
from jax.experimental import pallas as pl
from jax.experimental.pallas import tpu as pltpu
from jax.sharding import PartitionSpec as P

HEADS = 64
HEAD_DIM = 128
PRE_PAGES = 48
DEC_PAGES = 12
LOG2_SCALE = math.log2(math.e) / math.sqrt(HEAD_DIM)
PLANE = 4
MESH = pl.DeviceIdType.MESH
CONTRACT_LAST = (((1,), (1,)), ((), ()))


def scores_of(queries, keys):
    return lax.dot_general(queries, keys, CONTRACT_LAST, preferred_element_type=jnp.float32)


def weigh(score_parts, value_parts):
    highest = functools.reduce(
        jnp.maximum, [jnp.max(s, axis=1, keepdims=True) for s in score_parts]
    )
    total = 0.0
    summed = 0.0
    for scores, values in zip(score_parts, value_parts):
        terms = jnp.exp2((scores - highest) * LOG2_SCALE)
        total = total + jnp.sum(terms, axis=1, keepdims=True)
        summed = summed + jnp.dot(
            terms.astype(jnp.bfloat16), values, preferred_element_type=jnp.float32
        )
    return summed / total


def attention_kernel(
    places, prefix_length, context_length,
    queries, decode_queries, entries, decode_entries, pages, own_pages,
    output, decode_output, cache, sems,
):
    page_count, _, page_tokens, _ = cache.shape
    head = pl.program_id(0)
    row_count = queries.shape[0]
    group = queries.shape[1] // HEAD_DIM

    @pl.when(head == 0)
    def _():
        def fetch(sem, t, carry):
            place = places[t]

            @pl.when(place >= 0)
            def _():
                pltpu.make_async_copy(pages.at[place], cache.at[t], sem).start()

            @pl.when(place < 0)
            def _():
                pltpu.make_async_copy(own_pages.at[-1 - place], cache.at[t], sem).start()

            return carry

        lax.fori_loop(0, PRE_PAGES, functools.partial(fetch, sems.at[0]), 0)
        lax.fori_loop(PRE_PAGES, page_count, functools.partial(fetch, sems.at[1]), 0)
        prefix = cache.at[pl.ds(0, PRE_PAGES)]
        pltpu.make_async_copy(prefix, prefix, sems.at[0]).wait()

    columns = pl.ds(pl.multiple_of(head * HEAD_DIM, HEAD_DIM), HEAD_DIM)
    span = PRE_PAGES * page_tokens
    prefix_keys = cache[:PRE_PAGES, 0, :, columns].reshape(span, HEAD_DIM)
    prefix_values = cache[:PRE_PAGES, 1, :, columns].reshape(span, HEAD_DIM)
    position = lax.broadcasted_iota(jnp.int32, (1, span), 1)
    prefix_bias = jnp.where(position < prefix_length[0], 0.0, -jnp.inf)
    causal_bias = jnp.where(
        lax.broadcasted_iota(jnp.int32, (row_count, row_count), 0)
        >= lax.broadcasted_iota(jnp.int32, (row_count, row_count), 1),
        0.0,
        -jnp.inf,
    )
    own_keys = entries[0]
    own_values = entries[1]
    step = 4
    for start in range(0, group, step):
        stacked = jnp.concatenate(
            [queries[:, g * HEAD_DIM : (g + 1) * HEAD_DIM] for g in range(start, start + step)],
            axis=0,
        )
        own_scores = scores_of(stacked, own_keys).reshape(step, row_count, row_count)
        own_scores = (own_scores + causal_bias[None]).reshape(step * row_count, row_count)
        prefix_scores = scores_of(stacked, prefix_keys) + prefix_bias
        result = weigh([own_scores, prefix_scores], [own_values, prefix_values])
        result = result.astype(jnp.bfloat16)
        for g in range(step):
            output[:, (start + g) * HEAD_DIM : (start + g + 1) * HEAD_DIM] = result[
                g * row_count : (g + 1) * row_count
            ]

    @pl.when(head == 0)
    def _():
        context = cache.at[pl.ds(PRE_PAGES, page_count - PRE_PAGES)]
        pltpu.make_async_copy(context, context, sems.at[1]).wait()

    context_span = (page_count - PRE_PAGES) * page_tokens
    row_span = DEC_PAGES * page_tokens
    context_keys = cache[PRE_PAGES:, 0, :, columns].reshape(context_span, HEAD_DIM)
    context_values = cache[PRE_PAGES:, 1, :, columns].reshape(context_span, HEAD_DIM)
    row_queries = decode_queries[0]
    shape = (row_queries.shape[0], context_span)
    row = lax.broadcasted_iota(jnp.int32, shape, 0) // group
    place = lax.broadcasted_iota(jnp.int32, shape, 1)
    usable = jnp.zeros(shape, jnp.bool_)
    for r in range(context_span // row_span):
        usable = usable | (
            (row == r) & (place >= r * row_span) & (place < r * row_span + context_length[r])
        )
    context_scores = jnp.where(usable, scores_of(row_queries, context_keys), -jnp.inf)
    new_scores = scores_of(row_queries, decode_entries[0])
    own = lax.broadcasted_iota(jnp.int32, new_scores.shape, 0) // group
    own = own == lax.broadcasted_iota(jnp.int32, new_scores.shape, 1)
    new_scores = jnp.where(own, new_scores, -jnp.inf)
    decode_output[0] = weigh(
        [new_scores, context_scores], [decode_entries[1], context_values]
    ).astype(jnp.bfloat16)


def attention(places, prefix_length, context_length, queries, decode_queries, entries,
              decode_entries, pages, own_pages):
    row_count = queries.shape[0]
    decode_count = decode_queries.shape[0]
    key_heads = pages.shape[-1] // HEAD_DIM
    group = HEADS // key_heads
    page_count = places.shape[0]
    arranged = decode_queries.reshape(decode_count, key_heads, group, HEAD_DIM)
    arranged = jnp.transpose(arranged, (1, 0, 2, 3)).reshape(key_heads, -1, HEAD_DIM)
    padded = jnp.pad(decode_entries, ((0, 0), (0, -decode_count % 16), (0, 0)))
    output, decoded = pl.pallas_call(
        attention_kernel,
        grid_spec=pltpu.PrefetchScalarGridSpec(
            num_scalar_prefetch=3,
            grid=(key_heads,),
            in_specs=[
                pl.BlockSpec((row_count, group * HEAD_DIM), lambda h, *_: (0, h)),
                pl.BlockSpec((1,) + arranged.shape[1:], lambda h, *_: (h, 0, 0)),
                pl.BlockSpec((2, row_count, HEAD_DIM), lambda h, *_: (0, 0, h)),
                pl.BlockSpec((2, padded.shape[1], HEAD_DIM), lambda h, *_: (0, 0, h)),
                pl.BlockSpec(memory_space=pl.ANY),
                pl.BlockSpec(memory_space=pl.ANY),
            ],
            out_specs=[
                pl.BlockSpec((row_count, group * HEAD_DIM), lambda h, *_: (0, h)),
                pl.BlockSpec((1,) + arranged.shape[1:], lambda h, *_: (h, 0, 0)),
            ],
            scratch_shapes=[
                pltpu.VMEM((page_count,) + pages.shape[1:], pages.dtype),
                pltpu.SemaphoreType.DMA((2,)),
            ],
        ),
        out_shape=[
            jax.ShapeDtypeStruct(queries.shape, jnp.bfloat16),
            jax.ShapeDtypeStruct(arranged.shape, jnp.bfloat16),
        ],
        compiler_params=pltpu.CompilerParams(
            dimension_semantics=("arbitrary",), vmem_limit_bytes=40 * 1024 * 1024
        ),
        name="paged_attention",
    )(places, prefix_length, context_length, queries, arranged, entries, padded, pages, own_pages)
    decoded = decoded.reshape(key_heads, decode_count, group, HEAD_DIM)
    decoded = jnp.transpose(decoded, (1, 0, 2, 3)).reshape(decode_queries.shape)
    return output, decoded


def exchange_kernel(chunks, shared, served, held, far_send, far_recv, side_send, side_recv, core_send,
                    core_recv):
    plane_count = served.shape[0]
    me = lax.axis_index("pool")
    plane = me // PLANE
    within = me % PLANE
    side = within // 2
    core = within % 2
    side_device = plane * PLANE + (1 - side) * 2 + core
    core_device = plane * PLANE + side * 2 + (1 - core)

    barrier = pltpu.get_barrier_semaphore()
    for offset in range(1, plane_count):
        pl.semaphore_signal(
            barrier, inc=1,
            device_id={"pool": lax.rem(plane + offset, plane_count) * PLANE + within},
            device_id_type=MESH,
        )
    for device in (side_device, core_device):
        pl.semaphore_signal(barrier, inc=1, device_id={"pool": device}, device_id_type=MESH)
    pl.semaphore_wait(barrier, plane_count + 1)

    def far(offset, k):
        target = lax.rem(plane + offset, plane_count)
        return pltpu.make_async_remote_copy(
            src_ref=served.at[target, pl.ds(*chunks[k])],
            dst_ref=held.at[me, pl.ds(*chunks[k])],
            send_sem=far_send.at[offset, k],
            recv_sem=far_recv.at[offset, k],
            device_id={"pool": target * PLANE + within},
            device_id_type=MESH,
        )

    def spread(offset, k, other_side, to_core):
        source_plane = lax.rem(plane + plane_count - offset, plane_count)
        row = (1 - side) if other_side else side
        source = source_plane * PLANE + row * 2 + core
        if offset == 0 and not other_side:
            block = served.at[plane, pl.ds(*chunks[k])]
        else:
            block = held.at[source, pl.ds(*chunks[k])]
        if to_core:
            send, recv = core_send.at[int(other_side), offset, k], core_recv.at[int(other_side), offset, k]
        else:
            send, recv = side_send.at[offset, k], side_recv.at[offset, k]
        return pltpu.make_async_remote_copy(
            src_ref=block,
            dst_ref=held.at[source, pl.ds(*chunks[k])],
            send_sem=send,
            recv_sem=recv,
            device_id={"pool": core_device if to_core else side_device},
            device_id_type=MESH,
        )

    count = len(chunks)
    for k in range(count):
        for offset in range(1, plane_count):
            far(offset, k).start()
    for k in range(count):
        if k < shared:
            spread(0, k, False, False).start()
        spread(0, k, False, True).start()

    def forward(k):
        for offset in range(plane_count):
            spread(offset, k, False, False).wait_recv()
            spread(offset, k, True, True).start()

    for k in range(count):
        for offset in range(1, plane_count):
            far(offset, k).wait_recv()
            if k < shared:
                spread(offset, k, False, False).start()
            spread(offset, k, False, True).start()
        if 0 < k <= shared:
            forward(k - 1)
    if shared == count:
        forward(count - 1)
    for k in range(count):
        for offset in range(plane_count):
            if offset:
                far(offset, k).wait_send()
            spread(offset, k, False, True).wait()
            if k < shared:
                spread(offset, k, False, False).wait_send()
                spread(offset, k, True, True).wait()


def exchange(served, shared_length, pool_size, collective_id):
    plane_count, length = served.shape[:2]
    shared_length = min(shared_length, length)
    shared = max(1, min(5, 20 // plane_count, shared_length))
    edges = [shared_length * k // shared for k in range(shared + 1)]
    if length > shared_length:
        middle = (length + shared_length) // 2
        edges += [middle, length] if middle > shared_length else [length]
    chunks = [(low, high - low) for low, high in zip(edges, edges[1:])]
    pieces = len(chunks)
    one = pltpu.SemaphoreType.DMA((plane_count, pieces))
    two = pltpu.SemaphoreType.DMA((2, plane_count, pieces))
    return pl.pallas_call(
        functools.partial(exchange_kernel, chunks, shared),
        out_shape=jax.ShapeDtypeStruct((pool_size,) + served.shape[1:], served.dtype),
        in_specs=[pl.BlockSpec(memory_space=pl.ANY)],
        out_specs=pl.BlockSpec(memory_space=pl.ANY),
        scratch_shapes=[one, one, one, one, two, two],
        compiler_params=pltpu.CompilerParams(
            collective_id=collective_id, has_side_effects=True,
            vmem_limit_bytes=56 * 1024 * 1024,
        ),
        name="page_exchange",
    )(served)


def gather_kernel(slots, pages, served, sem):
    target = pl.program_id(0)

    def fetch(t, carry):
        pltpu.make_async_copy(pages.at[slots[target, t]], served.at[0, t], sem).start()
        return carry

    lax.fori_loop(0, served.shape[1], fetch, 0)
    pltpu.make_async_copy(served, served, sem).wait()


def gather(slots, pages):
    block = (1, slots.shape[1]) + pages.shape[1:]
    return pl.pallas_call(
        gather_kernel,
        grid_spec=pltpu.PrefetchScalarGridSpec(
            num_scalar_prefetch=1,
            grid=slots.shape[:1],
            in_specs=[pl.BlockSpec(memory_space=pl.ANY)],
            out_specs=pl.BlockSpec(block, lambda q, *_: (q, 0, 0, 0, 0)),
            scratch_shapes=[pltpu.SemaphoreType.DMA],
        ),
        out_shape=jax.ShapeDtypeStruct(slots.shape + pages.shape[1:], pages.dtype),
        compiler_params=pltpu.CompilerParams(
            dimension_semantics=("arbitrary",), vmem_limit_bytes=56 * 1024 * 1024
        ),
        name="gather_pages",
    )(slots, pages)


def tables_kernel(table, tables, local_sem, part_send, part_recv, far_send, far_recv, near_send,
                  near_recv):
    parts, plane_count = tables.shape[1:3]
    part = lax.axis_index("replica")
    me = lax.axis_index("pool")
    plane = me // PLANE
    within = me % PLANE

    def other_part(offset):
        return {"replica": lax.rem(part + offset, parts), "pool": me}

    def other_plane(offset):
        return {"pool": lax.rem(plane + offset, plane_count) * PLANE + within}

    def other_place(offset):
        return {"pool": plane * PLANE + lax.rem(within + offset, PLANE)}

    barrier = pltpu.get_barrier_semaphore()
    stages = [(other_part, parts), (other_plane, plane_count), (other_place, PLANE)]
    for device_of, size in stages:
        for offset in range(1, size):
            pl.semaphore_signal(
                barrier, inc=1, device_id=device_of(offset), device_id_type=MESH
            )
    pl.semaphore_wait(barrier, parts + plane_count + PLANE - 3)
    mine = pltpu.make_async_copy(table, tables.at[within, part, plane], local_sem)
    mine.start()
    mine.wait()
    blocks = [
        tables.at[within, part, plane],
        tables.at[within, pl.ds(0, parts), plane],
        tables.at[within],
    ]
    sems = [(part_send, part_recv), (far_send, far_recv), (near_send, near_recv)]
    for (device_of, size), block, (send, recv) in zip(stages, blocks, sems):
        copies = [
            pltpu.make_async_remote_copy(
                src_ref=block,
                dst_ref=block,
                send_sem=send.at[offset],
                recv_sem=recv.at[offset],
                device_id=device_of(offset),
                device_id_type=MESH,
            )
            for offset in range(1, size)
        ]
        for copy in copies:
            copy.start()
        for copy in copies:
            copy.wait()


def gather_tables(named, parts, plane_count, collective_id):
    width = -(-named.shape[0] // 128) * 128
    table = jnp.pad(named, (0, width - named.shape[0]), constant_values=-1)[None, :]
    sems = [pltpu.SemaphoreType.DMA]
    for size in (parts, plane_count, PLANE):
        sems += [pltpu.SemaphoreType.DMA((size,))] * 2
    return pl.pallas_call(
        tables_kernel,
        out_shape=jax.ShapeDtypeStruct((PLANE, parts, plane_count, 1, width), jnp.int32),
        in_specs=[pl.BlockSpec(memory_space=pltpu.VMEM)],
        out_specs=pl.BlockSpec(memory_space=pltpu.VMEM),
        scratch_shapes=sems,
        compiler_params=pltpu.CompilerParams(
            collective_id=collective_id, has_side_effects=True
        ),
        name="gather_tables",
    )(table)


def on_device(
    stretch_queries,
    decode_queries,
    stretch_entries,
    decode_entries,
    pool_pages,
    page_owner,
    page_slot,
    prefix_length,
    context_length,
):
    pool_size = lax.axis_size("pool")
    parts = lax.axis_size("replica")
    part = lax.axis_index("replica")
    me = lax.axis_index("pool")
    plane_count = pool_size // PLANE
    page_count = page_slot.shape[0]
    slot_count, _, page_tokens, _ = pool_pages.shape
    capacity = max(2, 4 * page_count // (3 * pool_size))
    longest = min(slot_count, PLANE * capacity)

    first = jnp.concatenate(
        [jnp.arange(PRE_PAGES), jnp.tile(jnp.arange(DEC_PAGES), context_length.shape[0])]
    ).astype(jnp.int32) * page_tokens
    limit = jnp.concatenate(
        [
            jnp.broadcast_to(prefix_length, (PRE_PAGES,)),
            jnp.repeat(context_length, DEC_PAGES),
        ]
    )
    named = jnp.where(first < limit, page_owner[:, 0] * slot_count + page_slot, -1)
    everyone = gather_tables(named, parts, plane_count, 0)
    everyone = jnp.transpose(everyone, (1, 2, 0, 3, 4))
    everyone = everyone.reshape(parts * plane_count * 2, -1, 1)
    every_page = jnp.arange(pool_size * slot_count, dtype=jnp.int32)
    by_side = jnp.any(everyone == every_page, axis=1)
    by_side = by_side.reshape(parts, plane_count, 2, pool_size, slot_count)
    needed = (by_side[:, :, 0] | by_side[:, :, 1]).astype(jnp.int32)
    most = jnp.max(jnp.sum(needed, axis=-1))
    by_side = lax.dynamic_index_in_dim(by_side, part, 0, keepdims=False).astype(jnp.int32)
    source_side = (jnp.arange(pool_size)[:, None] // 2) % 2
    early = jnp.where(source_side == 0, by_side[:, 1], by_side[:, 0])
    late = jnp.maximum(by_side[:, 0], by_side[:, 1]) - early

    def ranked(early, late):
        early_rank = jnp.cumsum(early, axis=1) - 1
        late_rank = jnp.cumsum(late, axis=1) - 1 + jnp.sum(early, axis=1, keepdims=True)
        return jnp.where(early == 1, early_rank, jnp.where(late == 1, late_rank, -1))

    asked_rank = ranked(
        lax.dynamic_index_in_dim(early, me, 1, keepdims=False),
        lax.dynamic_index_in_dim(late, me, 1, keepdims=False),
    )
    plane = me // PLANE
    coming_rank = ranked(
        lax.dynamic_index_in_dim(early, plane, 0, keepdims=False),
        lax.dynamic_index_in_dim(late, plane, 0, keepdims=False),
    ).reshape(-1)
    rank = jnp.sum(
        jnp.where(named[:, None] == every_page[None, :], coming_rank[None, :], 0), axis=1
    )
    slot_index = jnp.arange(slot_count, dtype=jnp.int32)
    slots = jnp.sum(
        jnp.where(
            asked_rank[:, None, :] == jnp.arange(longest, dtype=jnp.int32)[None, :, None],
            slot_index[None, None, :],
            0,
        ),
        axis=2,
    )
    lengths = sorted({-(-longest * share // 32) for share in (20, 21, 22, 24, 32)})

    def finish(length, collective_id):
        served = gather(slots[:, :length], pool_pages)
        held = exchange(served, 2 * capacity, pool_size, collective_id)
        held = held.reshape((pool_size * length,) + pool_pages.shape[1:])
        owner = page_owner[:, 0]
        places = jnp.where(owner == me, -1 - page_slot, owner * length + rank)
        places = jnp.where(named >= 0, places, -1)
        return attention(
            places, prefix_length, context_length, stretch_queries, decode_queries,
            stretch_entries, decode_entries, held, pool_pages,
        )

    choice = sum((most > length).astype(jnp.int32) for length in lengths[:-1])
    return lax.switch(
        choice,
        [functools.partial(finish, length, index + 1) for index, length in enumerate(lengths)],
    )


def solution(mesh):
    rows = P(("replica", "pool"), None)
    entries = P(None, ("replica", "pool"), None)
    vector = P(("replica", "pool"))
    pages = P(("replica", "pool"), None, None, None)
    return jax.shard_map(
        on_device,
        mesh=mesh,
        in_specs=(rows, rows, entries, entries, pages, rows, vector, vector, vector),
        out_specs=(rows, rows),
        check_vma=False,
    )
```
